32 devices in a mesh: space: 4 (over x, core), chaos: 8 (over z, y).
Axes of the slice: x: 2, y: 2, z: 4, core: 2. Of those that a mesh axis runs over, the one named last changes fastest.
Arguments:
- chaos_field: bfloat16 [256, 32, 16, 128], P('chaos', 'space'), may hold values from -6 to 6
- conductivity: float32 [11, 32, 16, 128], P(None, 'space', 'chaos'), may hold values from 0.1 to 1
- triple_tensor: bfloat16 [11, 256, 256], replicated, may hold values from -0.02734375 to 0.02734375
- block_pattern: int32 [8, 8], replicated, may hold values 0 or 1
Outputs:
- first: bfloat16 [256, 32, 16, 128], P('chaos', 'space')
- second: bfloat16 [256, 32, 16, 128], P('chaos', 'space')
The draws below stay inside these ranges and needn't reach their ends.
All inputs are finite; a program needn't handle non-finite values.
Results may differ from the reference program's by a relative error of at most 0.0043.
Values may be sent and summed in bfloat16 or wider, within the bound.
A program may use at most 128 MiB of HBM per device.

```python
import math
import jax
import jax.numpy as jnp
from jax import lax

P_SIZE = 256
K = 11
BLK = 32
NY = 16
NZ = 128
NB = 8
NX = 32


def with_ends(entries, key, smallest, top_value):
    spot = [jax.random.randint(jax.random.fold_in(key, axis), (), 0, length) for axis, length in enumerate(entries.shape)]
    longest = entries.shape.index(max(entries.shape))
    beside = spot[:longest] + [(spot[longest] + 1) % entries.shape[longest]] + spot[longest + 1:]
    return entries.at[tuple(spot)].set(smallest).at[tuple(beside)].set(top_value)


def level_of(own_key, shape, pieces, least, largest):
    def one(position, blocks):
        heights = jax.random.uniform(jax.random.fold_in(jax.random.fold_in(own_key, 6), position), (blocks,), jnp.float32, least / len(pieces), largest / len(pieces))
        return jnp.repeat(jnp.exp(heights), shape[position] // blocks).reshape((-1,) + (1,) * (len(shape) - position - 1))

    gain = one(*pieces[0])
    for cut in pieces[1:]:
        gain = gain * one(*cut)
    return gain


def bell_draw(key, dims, deviation, most, split=(), held_as=jnp.bfloat16):
    gain = level_of(key, dims, split, -0.22, 0.18) if split else 1.0
    drawn = jax.random.normal(key, dims, jnp.float32) * deviation * gain
    return jnp.minimum(jnp.maximum(drawn, -most), most).astype(held_as)


def setup_inputs(seed: int = 0) -> dict:
    key_of = jax.random.split(jax.random.key(seed), 5)
    return {
        "chaos_field": bell_draw(key_of[0], (P_SIZE, NX, NY, NZ), 1.0, 6.0, ((0, 8), (1, 4))),
        "conductivity": jnp.clip(jnp.exp(math.log(1.0) - 2.3025851 * jax.random.uniform(key_of[1], (K, NX, NY, NZ), jnp.float32) ** level_of(key_of[1], (K, NX, NY, NZ), ((1, 4), (2, 8)), -0.2, 0.2)), 0.1, 1.0),
        "triple_tensor": bell_draw(key_of[2], (K, P_SIZE, P_SIZE), (16 * K * P_SIZE) ** -0.5, 0.02734375),
        "block_pattern": with_ends((jax.random.randint(key_of[3], (NB, NB), 0, 3) < 2).astype(jnp.int32), jax.random.fold_in(key_of[3], 1), 0, 1),
    }


def neighbours(padded):
    centre = padded[..., 1:-1, :, :]
    lead = [(0, 0)] * (centre.ndim - 2)
    ypad = jnp.pad(centre, lead + [(1, 1), (0, 0)])
    zpad = jnp.pad(centre, lead + [(0, 0), (1, 1)])
    return centre, [padded[..., :-2, :, :], padded[..., 2:, :, :], ypad[..., :-2, :], ypad[..., 2:, :], zpad[..., :-2], zpad[..., 2:]]


def reference(chaos_field, conductivity, triple_tensor, block_pattern):
    expanded = jnp.repeat(jnp.repeat(block_pattern, BLK, 0), BLK, 1).astype(triple_tensor.dtype)
    masked = (triple_tensor * expanded[None]).astype(jnp.float32)
    kpad = jnp.pad(conductivity, ((0, 0), (1, 1), (0, 0), (0, 0)))
    kcentre, knear = neighbours(kpad)
    faces = jnp.stack([0.5 * (kcentre + other) for other in knear])
    face_total = jnp.sum(faces, axis=0)

    def matvec(field):
        values = field.astype(jnp.float32)

        def one_mode(k, acc):
            mixed = jnp.einsum("ij,jxyz->ixyz", masked[k], values, precision=lax.Precision.HIGHEST)
            padded = jnp.pad(mixed, ((0, 0), (1, 1), (0, 0), (0, 0)))
            centre, near = neighbours(padded)
            result = face_total[k] * centre
            for index in range(6):
                result = result - faces[index, k] * near[index]
            return acc + result

        return lax.fori_loop(0, K, one_mode, jnp.zeros(values.shape, jnp.float32))

    first = matvec(chaos_field).astype(jnp.bfloat16)
    second = matvec(first).astype(jnp.bfloat16)
    return first, second
```

```python
import functools

import jax
import jax.numpy as jnp
from jax import lax
from jax.experimental import pallas as pl
from jax.experimental.pallas import tpu as pltpu
from jax.sharding import PartitionSpec as P

MESH = pl.DeviceIdType.MESH
TILE = 64


def kernel(
    n, slabs, modes, vt, tensor, mask, kt, out1, out2,
    vbuf, fbuf, sbuf, kbuf, skap, m2, acc, w, wy,
    in_send, in_recv, khalo_send, khalo_recv, vhalo_send, vhalo_recv, fhalo_send, fhalo_recv,
    out_send, out_recv, local_sem,
):
    me = lax.axis_index("chaos")
    sp = lax.axis_index("space")
    yl, nx = vbuf.shape[0] - 2, vbuf.shape[1] - 2
    coeffs, nz = vbuf.shape[2], vbuf.shape[3]
    cl = coeffs // n
    tiles = coeffs // TILE
    f32, bf16 = jnp.float32, jnp.bfloat16

    down, up = me > 0, me < n - 1
    left, right = sp > 0, sp < slabs - 1

    for buf in (vbuf, fbuf, kbuf):
        @pl.when(jnp.logical_not(down))
        def _(buf=buf):
            buf[0] = jnp.zeros(buf.shape[1:], buf.dtype)

        @pl.when(jnp.logical_not(up))
        def _(buf=buf):
            buf[yl + 1] = jnp.zeros(buf.shape[1:], buf.dtype)

        @pl.when(jnp.logical_not(left))
        def _(buf=buf):
            for y in range(yl):
                buf[1 + y, 0] = jnp.zeros(buf.shape[2:], buf.dtype)

        @pl.when(jnp.logical_not(right))
        def _(buf=buf):
            for y in range(yl):
                buf[1 + y, nx + 1] = jnp.zeros(buf.shape[2:], buf.dtype)

    for y in range(yl):
        for x in range(nx):
            kbuf[1 + y, 1 + x] = kt[y, x]

    barrier = pltpu.get_barrier_semaphore()

    @pl.loop(1, n)
    def _(s):
        pl.semaphore_signal(barrier, inc=1, device_id={"chaos": lax.rem(me + s, n)}, device_id_type=MESH)

    @pl.when(left)
    def _():
        pl.semaphore_signal(barrier, inc=1, device_id={"space": sp - 1}, device_id_type=MESH)

    @pl.when(right)
    def _():
        pl.semaphore_signal(barrier, inc=1, device_id={"space": sp + 1}, device_id_type=MESH)

    pl.semaphore_wait(barrier, n - 1 + left.astype(jnp.int32) + right.astype(jnp.int32))

    def in_copy(d, src_dev, peer):
        return pltpu.make_async_remote_copy(
            src_ref=vt.at[pl.ds(d * yl, yl)],
            dst_ref=vbuf.at[pl.ds(1, yl), pl.ds(1, nx), pl.ds(pl.multiple_of(src_dev * cl, cl), cl)],
            send_sem=in_send.at[d], recv_sem=in_recv.at[src_dev],
            device_id={"chaos": peer}, device_id_type=MESH,
        )

    @pl.loop(1, n)
    def _(s):
        d = lax.rem(me + s, n)
        in_copy(d, me, d).start()

    own_in = pltpu.make_async_copy(
        vt.at[pl.ds(me * yl, yl)],
        vbuf.at[pl.ds(1, yl), pl.ds(1, nx), pl.ds(pl.multiple_of(me * cl, cl), cl)],
        local_sem.at[0],
    )
    own_in.start()

    inner, rows = pl.ds(1, nx), pl.ds(1, yl)
    other = lax.rem(me + 1, n)

    def halo(buf, send, recv, index, target, xs=None):
        at = inner if xs is None else xs
        if index == 0:
            src, dst = buf.at[1, at], buf.at[yl + 1, at]
        elif index == 1:
            src, dst = buf.at[yl, at], buf.at[0, at]
        elif index == 2:
            src, dst = buf.at[rows, 1], buf.at[rows, nx + 1]
        else:
            src, dst = buf.at[rows, nx], buf.at[rows, 0]
        return pltpu.make_async_remote_copy(
            src_ref=src, dst_ref=dst, send_sem=send.at[index], recv_sem=recv.at[index],
            device_id=target, device_id_type=MESH,
        )

    sends = [
        (down, {"chaos": me - 1}), (up, {"chaos": me + 1}),
        (left, {"space": sp - 1}), (right, {"space": sp + 1}),
    ]
    arrives = [up, down, right, left]

    def halo_start(buf, send, recv, index, xs=None):
        cond, target = sends[index]

        @pl.when(cond)
        def _():
            halo(buf, send, recv, index, target, xs).start()

    def halo_wait_recv(buf, send, recv):
        for index in range(4):
            @pl.when(arrives[index])
            def _(index=index):
                halo(buf, send, recv, index, {"chaos": other}).wait_recv()

    def halo_wait_send(buf, send, recv):
        for index in range(4):
            @pl.when(sends[index][0])
            def _(index=index):
                halo(buf, send, recv, index, {"chaos": other}).wait_send()

    for index in range(4):
        halo_start(kbuf, khalo_send, khalo_recv, index)

    @pl.loop(0, tiles)
    def _(it):
        at = pl.ds(pl.multiple_of(it * TILE, TILE), TILE)
        part = mask[at]
        for k in range(modes):
            value = tensor[k, at] * part
            m2[it, k * TILE:(k + 1) * TILE, :coeffs] = value
            m2[it, k * TILE:(k + 1) * TILE, coeffs:] = value

    lane = lax.broadcasted_iota(jnp.int32, (1, nz), 1)

    def zsum(block):
        before = jnp.where(lane == 0, 0.0, pltpu.roll(block, 1, 1))
        after = jnp.where(lane == nz - 1, 0.0, pltpu.roll(block, nz - 1, 1))
        return before + after

    def row(buf, x, first=1):
        return jnp.concatenate([buf[first + y, x] for y in range(yl)], axis=1)

    halo_wait_recv(kbuf, khalo_send, khalo_recv)

    @pl.loop(0, nx)
    def _(x):
        parts = []
        for y in range(yl):
            parts.append(
                kbuf[1 + y, x] + kbuf[1 + y, x + 2] + kbuf[y, x + 1] + kbuf[y + 2, x + 1]
                + zsum(kbuf[1 + y, x + 1])
            )
        skap[x] = jnp.concatenate(parts, axis=1)

    def at_tile(it):
        return pl.ds(pl.multiple_of(it * TILE, TILE), TILE)

    def weighted(products, weights):
        total = products[:TILE] * weights[0:1]
        for k in range(1, modes):
            total = total + products[k * TILE:(k + 1) * TILE] * weights[k:k + 1]
        return total

    def mix(it, operand):
        return jnp.dot(m2[it, :, :operand.shape[0]], operand, preferred_element_type=f32)

    def interior(buf):
        @pl.loop(0, nx)
        def _(x):
            field, kap, sk = row(buf, x + 1), row(kbuf, x + 1), skap[x]

            @pl.loop(0, tiles)
            def _(it):
                products = mix(it, field)
                acc[x, at_tile(it)] = weighted(products, sk)
                w[x + 1, at_tile(it)] = weighted(products, kap)

    def borders(buf):
        for x in (0, nx + 1):
            field, kap = row(buf, x), row(kbuf, x)

            @pl.loop(0, tiles)
            def _(it, x=x, field=field, kap=kap):
                w[x, at_tile(it)] = weighted(mix(it, field), kap)

        @pl.loop(0, nx)
        def _(x):
            field = jnp.concatenate([buf[0, x + 1], buf[yl + 1, x + 1]], axis=1)
            kap = jnp.concatenate([kbuf[0, x + 1], kbuf[yl + 1, x + 1]], axis=1)

            @pl.loop(0, tiles)
            def _(it):
                wy[x, at_tile(it)] = weighted(mix(it, field), kap)

    def finish(buf, x, store):
        parts = []
        for y in range(yl):
            centre = buf[1 + y, x + 1].astype(f32)
            near = (
                buf[1 + y, x].astype(f32) + buf[1 + y, x + 2].astype(f32)
                + buf[y, x + 1].astype(f32) + buf[y + 2, x + 1].astype(f32)
            )
            parts.append(6.0 * centre - (near + zsum(centre)))
        lap = jnp.concatenate(parts, axis=1)
        high = lap.astype(bf16)
        low = (lap - high.astype(f32)).astype(bf16)
        both = jnp.concatenate([high, low], axis=0)
        kap = row(kbuf, x + 1)

        @pl.loop(0, tiles)
        def _(it):
            at = at_tile(it)
            total = acc[x, at] + weighted(mix(it, both), kap)
            total = total - (w[x, at] + w[x + 2, at])
            centre = w[x + 1, at]
            sides = wy[x, at]
            for y in range(yl):
                here = slice(y * nz, (y + 1) * nz)
                below = sides[:, :nz] if y == 0 else centre[:, (y - 1) * nz:y * nz]
                above = sides[:, nz:] if y == yl - 1 else centre[:, (y + 1) * nz:(y + 2) * nz]
                value = total[:, here] - (below + above + zsum(centre[:, here]))
                store(y, at, (0.5 * value).astype(bf16))

    def out_copy(which, src, out, d, src_dev, peer, srcx, dstx):
        return pltpu.make_async_remote_copy(
            src_ref=src(srcx, pl.ds(pl.multiple_of(d * cl, cl), cl)),
            dst_ref=out.at[pl.ds(src_dev * yl, yl), dstx],
            send_sem=out_send.at[which, d], recv_sem=out_recv.at[which, src_dev],
            device_id={"chaos": peer}, device_id_type=MESH,
        )

    def own_copy(which, src, out, srcx, dstx):
        return pltpu.make_async_copy(
            src(srcx, pl.ds(pl.multiple_of(me * cl, cl), cl)),
            out.at[pl.ds(me * yl, yl), dstx],
            local_sem.at[1 + which],
        )

    def out_start(which, src, out, srcx, dstx):
        @pl.loop(1, n)
        def _(s):
            d = lax.rem(me + s, n)
            out_copy(which, src, out, d, me, d, srcx, dstx).start()

        own_copy(which, src, out, srcx, dstx).start()

    def out_wait(which, src, out, srcx, dstx):
        @pl.loop(1, n)
        def _(s):
            d = lax.rem(me + s, n)
            copy = out_copy(which, src, out, d, d, d, srcx, dstx)
            copy.wait_send()
            copy.wait_recv()

        own_copy(which, src, out, srcx, dstx).wait()

    def first_at(xs, cs):
        return fbuf.at[rows, xs, cs]

    def second_at(xs, cs):
        return sbuf.at[:, xs, cs]

    @pl.loop(1, n)
    def _(s):
        d = lax.rem(me + s, n)
        in_copy(d, d, d).wait_recv()

    own_in.wait()
    for index in range(4):
        halo_start(vbuf, vhalo_send, vhalo_recv, index)
    interior(vbuf)
    halo_wait_recv(vbuf, vhalo_send, vhalo_recv)
    borders(vbuf)

    @pl.loop(0, nx)
    def _(x):
        def store(y, at, value):
            fbuf[1 + y, x + 1, at] = value

        finish(vbuf, x, store)
        for index in range(2):
            halo_start(fbuf, fhalo_send, fhalo_recv, index, x + 1)

        @pl.when(x == 0)
        def _():
            halo_start(fbuf, fhalo_send, fhalo_recv, 2)

        @pl.when(x == nx - 1)
        def _():
            halo_start(fbuf, fhalo_send, fhalo_recv, 3)

        out_start(0, first_at, out1, x + 1, x)

    interior(fbuf)
    halo_wait_recv(fbuf, fhalo_send, fhalo_recv)
    borders(fbuf)

    @pl.loop(0, nx)
    def _(x):
        def store(y, at, value):
            sbuf[y, x, at] = value

        finish(fbuf, x, store)
        out_start(1, second_at, out2, x, x)

    @pl.loop(1, n)
    def _(s):
        d = lax.rem(me + s, n)
        in_copy(d, d, d).wait_send()

    halo_wait_send(kbuf, khalo_send, khalo_recv)
    halo_wait_send(vbuf, vhalo_send, vhalo_recv)
    halo_wait_send(fbuf, fhalo_send, fhalo_recv)
    out_wait(0, first_at, out1, inner, pl.ds(0, nx))
    out_wait(1, second_at, out2, pl.ds(0, nx), pl.ds(0, nx))


def local(n, slabs, chaos_field, conductivity, triple_tensor, block_pattern):
    cl, nx, ny, nz = chaos_field.shape
    modes, coeffs, _ = triple_tensor.shape
    yl = ny // n
    kpad = -(-modes // 8) * 8
    block = coeffs // block_pattern.shape[0]
    f32, bf16 = jnp.float32, jnp.bfloat16
    mask = jnp.repeat(jnp.repeat(block_pattern, block, 0), block, 1).astype(bf16)
    vt = jnp.transpose(chaos_field, (2, 1, 0, 3))
    kt = jnp.pad(jnp.transpose(conductivity, (2, 1, 0, 3)), ((0, 0), (0, 0), (0, kpad - modes), (0, 0)))
    dma, vmem = pltpu.SemaphoreType.DMA, pltpu.VMEM
    out = jax.ShapeDtypeStruct((ny, nx, cl, nz), bf16)
    whole = pl.BlockSpec(memory_space=pltpu.VMEM)
    anywhere = pl.BlockSpec(memory_space=pl.ANY)
    first, second = pl.pallas_call(
        functools.partial(kernel, n, slabs, modes),
        out_shape=(out, out),
        in_specs=[anywhere, whole, whole, whole],
        out_specs=(anywhere, anywhere),
        scratch_shapes=[
            vmem((yl + 2, nx + 2, coeffs, nz), bf16),
            vmem((yl + 2, nx + 2, coeffs, nz), bf16),
            vmem((yl, nx, coeffs, nz), bf16),
            vmem((yl + 2, nx + 2, kpad, nz), f32),
            vmem((nx, kpad, yl * nz), f32),
            vmem((coeffs // TILE, modes * TILE, 2 * coeffs), bf16),
            vmem((nx, coeffs, yl * nz), f32),
            vmem((nx + 2, coeffs, yl * nz), f32),
            vmem((nx, coeffs, 2 * nz), f32),
            dma((n,)), dma((n,)),
            dma((4,)), dma((4,)), dma((4,)), dma((4,)), dma((4,)), dma((4,)),
            dma((2, n)), dma((2, n)), dma((3,)),
        ],
        compiler_params=pltpu.CompilerParams(
            collective_id=0, has_side_effects=True, vmem_limit_bytes=48 * 1024 * 1024,
        ),
    )(vt, triple_tensor, mask, kt)
    return jnp.transpose(first, (2, 1, 0, 3)), jnp.transpose(second, (2, 1, 0, 3))


def solution(mesh):
    n, slabs = mesh.shape["chaos"], mesh.shape["space"]
    return jax.shard_map(
        functools.partial(local, n, slabs),
        mesh=mesh,
        in_specs=(P("chaos", "space", None, None), P(None, "space", "chaos", None), P(), P()),
        out_specs=(P("chaos", "space", None, None), P("chaos", "space", None, None)),
        check_vma=False,
    )
```

```python
import functools

import jax
import jax.numpy as jnp
from jax import lax
from jax.experimental import pallas as pl
from jax.experimental.pallas import tpu as pltpu
from jax.sharding import PartitionSpec as P

MESH = pl.DeviceIdType.MESH
TILE = 64
BANDS = 4


def kernel(
    n, slabs, modes, vt, tensor, mask, kt, out1, out2,
    vbuf, fbuf, sbuf, kbuf, skap, m2, acc, w, wy,
    in_send, in_recv, own_sem, kx_send, kx_recv, ky_send, ky_recv, vy_send, vy_recv, fy_send, fy_recv,
    kh_send, kh_recv, vh_send, vh_recv, fh_send, fh_recv, out_send, out_recv, local_sem,
):
    me = lax.axis_index("chaos")
    sp = lax.axis_index("space")
    yl, nx = vbuf.shape[0] - 2, vbuf.shape[1] - 2
    coeffs, nz = vbuf.shape[2], vbuf.shape[3]
    cl = coeffs // n
    group = n // BANDS
    krows = kt.shape[0]
    tiles = coeffs // TILE
    f32, bf16 = jnp.float32, jnp.bfloat16
    band, part = me // group, me % group
    gx = sp * group + part
    down, up = band > 0, band < BANDS - 1
    left, right = gx > 0, gx < slabs * group - 1
    lx, rx = jnp.maximum(gx - 1, 0), gx + 1
    left_peer = {"space": lx // group, "chaos": band * group + lx % group}
    right_peer = {"space": rx // group, "chaos": band * group + rx % group}
    inner, rows = pl.ds(1, nx), pl.ds(1, yl)
    other = lax.rem(me + 1, n)

    for buf in (vbuf, fbuf, kbuf):
        @pl.when(jnp.logical_not(down))
        def _(buf=buf):
            buf[0] = jnp.zeros(buf.shape[1:], buf.dtype)

        @pl.when(jnp.logical_not(up))
        def _(buf=buf):
            buf[yl + 1] = jnp.zeros(buf.shape[1:], buf.dtype)

        @pl.when(jnp.logical_not(left))
        def _(buf=buf):
            for y in range(yl):
                buf[1 + y, 0] = jnp.zeros(buf.shape[2:], buf.dtype)

        @pl.when(jnp.logical_not(right))
        def _(buf=buf):
            for y in range(yl):
                buf[1 + y, nx + 1] = jnp.zeros(buf.shape[2:], buf.dtype)

    far_left = jnp.logical_and(left, part == 0)
    far_right = jnp.logical_and(right, part == group - 1)
    barrier = pltpu.get_barrier_semaphore()

    @pl.loop(1, n)
    def _(s):
        pl.semaphore_signal(barrier, inc=1, device_id={"chaos": lax.rem(me + s, n)}, device_id_type=MESH)

    for cond, peer in ((far_left, left_peer), (far_right, right_peer)):
        @pl.when(cond)
        def _(peer=peer):
            pl.semaphore_signal(barrier, inc=1, device_id=peer, device_id_type=MESH)

    pl.semaphore_wait(barrier, n - 1 + far_left.astype(jnp.int32) + far_right.astype(jnp.int32))

    def k_copy(p, src_part, peer):
        return pltpu.make_async_remote_copy(
            src_ref=kt.at[:, pl.ds(p * nx, nx)],
            dst_ref=kbuf.at[pl.ds(1 + src_part * krows, krows), inner],
            send_sem=kx_send.at[p], recv_sem=kx_recv.at[src_part],
            device_id={"chaos": peer}, device_id_type=MESH,
        )

    own_k = pltpu.make_async_copy(
        kt.at[:, pl.ds(part * nx, nx)], kbuf.at[pl.ds(1 + part * krows, krows), inner], local_sem.at[0],
    )
    own_k.start()

    @pl.loop(1, group)
    def _(s):
        p = lax.rem(part + s, group)
        k_copy(p, part, band * group + p).start()

    def my_rows(device):
        return pl.ds(pl.multiple_of(device * cl, cl), cl)

    def in_copy(d, src_dev, x):
        return pltpu.make_async_remote_copy(
            src_ref=vt.at[pl.ds((d // group) * yl, yl), (d % group) * nx + x],
            dst_ref=vbuf.at[rows, 1 + x, my_rows(src_dev)],
            send_sem=in_send.at[x, d], recv_sem=in_recv.at[x, src_dev],
            device_id={"chaos": d}, device_id_type=MESH,
        )

    def own_in(x):
        return pltpu.make_async_copy(
            vt.at[pl.ds(band * yl, yl), part * nx + x], vbuf.at[rows, 1 + x, my_rows(me)], own_sem.at[x],
        )

    @pl.loop(0, nx)
    def _(x):
        @pl.loop(1, n)
        def _(s):
            in_copy(lax.rem(me + s, n), me, x).start()

        own_in(x).start()

    def y_halo(buf, send, recv, index, target, xs, slot):
        src, dst = ((1, yl + 1), (yl, 0))[index]
        return pltpu.make_async_remote_copy(
            src_ref=buf.at[src, xs], dst_ref=buf.at[dst, xs],
            send_sem=send.at[index, slot], recv_sem=recv.at[index, slot],
            device_id=target, device_id_type=MESH,
        )

    def x_halo(buf, send, recv, index, target):
        src, dst = ((1, nx + 1), (nx, 0))[index]
        return pltpu.make_async_remote_copy(
            src_ref=buf.at[rows, src], dst_ref=buf.at[rows, dst],
            send_sem=send.at[index], recv_sem=recv.at[index],
            device_id=target, device_id_type=MESH,
        )

    y_sends = ((down, {"chaos": me - group}), (up, {"chaos": me + group}))
    x_sends = ((left, left_peer), (right, right_peer))
    y_arrives, x_arrives = (up, down), (right, left)

    def y_start(buf, send, recv, xs, slot):
        for index, (cond, target) in enumerate(y_sends):
            @pl.when(cond)
            def _(index=index, target=target):
                y_halo(buf, send, recv, index, target, xs, slot).start()

    def y_wait(buf, send, recv, xs, slot):
        for index, cond in enumerate(y_arrives):
            @pl.when(cond)
            def _(index=index):
                y_halo(buf, send, recv, index, {"chaos": other}, xs, slot).wait_recv()

    def y_sent(buf, send, recv, xs, slot):
        for index, (cond, _) in enumerate(y_sends):
            @pl.when(cond)
            def _(index=index):
                y_halo(buf, send, recv, index, {"chaos": other}, xs, slot).wait_send()

    def x_start(buf, send, recv, index, also=True):
        cond, target = x_sends[index]

        @pl.when(jnp.logical_and(cond, also))
        def _():
            x_halo(buf, send, recv, index, target).start()

    def x_wait(buf, send, recv, index):
        @pl.when(x_arrives[index])
        def _():
            x_halo(buf, send, recv, index, {"chaos": other}).wait_recv()

    def x_sent(buf, send, recv):
        for index in range(2):
            @pl.when(x_sends[index][0])
            def _(index=index):
                x_halo(buf, send, recv, index, {"chaos": other}).wait_send()

    own_k.wait()

    @pl.loop(1, group)
    def _(s):
        p = lax.rem(part + s, group)
        k_copy(p, p, band * group + p).wait_recv()

    y_start(kbuf, ky_send, ky_recv, inner, 0)
    for index in range(2):
        x_start(kbuf, kh_send, kh_recv, index)

    @pl.loop(0, tiles)
    def _(it):
        at = pl.ds(pl.multiple_of(it * TILE, TILE), TILE)
        kept = mask[at]
        for k in range(modes):
            value = tensor[k, at] * kept
            m2[it, k * TILE:(k + 1) * TILE, :coeffs] = value
            m2[it, k * TILE:(k + 1) * TILE, coeffs:] = value

    lane = lax.broadcasted_iota(jnp.int32, (1, nz), 1)

    def zsum(block):
        before = jnp.where(lane == 0, 0.0, pltpu.roll(block, 1, 1))
        after = jnp.where(lane == nz - 1, 0.0, pltpu.roll(block, nz - 1, 1))
        return before + after

    def row(buf, x, first=1):
        return jnp.concatenate([buf[first + y, x] for y in range(yl)], axis=1)

    y_wait(kbuf, ky_send, ky_recv, inner, 0)
    for index in range(2):
        x_wait(kbuf, kh_send, kh_recv, index)

    @pl.loop(0, nx)
    def _(x):
        parts = []
        for y in range(yl):
            parts.append(
                kbuf[1 + y, x] + kbuf[1 + y, x + 2] + kbuf[y, x + 1] + kbuf[y + 2, x + 1]
                + zsum(kbuf[1 + y, x + 1])
            )
        skap[x] = jnp.concatenate(parts, axis=1)

    def at_tile(it):
        return pl.ds(pl.multiple_of(it * TILE, TILE), TILE)

    def weighted(products, weights):
        total = products[:TILE] * weights[0:1]
        for k in range(1, modes):
            total = total + products[k * TILE:(k + 1) * TILE] * weights[k:k + 1]
        return total

    def mix(it, operand):
        return jnp.dot(m2[it, :, :operand.shape[0]], operand, preferred_element_type=f32)

    def interior(buf, x):
        field, kap, sk = row(buf, x + 1), row(kbuf, x + 1), skap[x]

        @pl.loop(0, tiles, unroll=True)
        def _(it):
            products = mix(it, field)
            acc[x, at_tile(it)] = weighted(products, sk)
            w[x + 1, at_tile(it)] = weighted(products, kap)

    def x_border(buf, x):
        field, kap = row(buf, x), row(kbuf, x)

        @pl.loop(0, tiles, unroll=True)
        def _(it):
            w[x, at_tile(it)] = weighted(mix(it, field), kap)

    def y_border(buf, x):
        field = jnp.concatenate([buf[0, x + 1], buf[yl + 1, x + 1]], axis=1)
        kap = jnp.concatenate([kbuf[0, x + 1], kbuf[yl + 1, x + 1]], axis=1)

        @pl.loop(0, tiles, unroll=True)
        def _(it):
            wy[x, at_tile(it)] = weighted(mix(it, field), kap)

    def finish(buf, x, store):
        parts = []
        for y in range(yl):
            centre = buf[1 + y, x + 1].astype(f32)
            near = (
                buf[1 + y, x].astype(f32) + buf[1 + y, x + 2].astype(f32)
                + buf[y, x + 1].astype(f32) + buf[y + 2, x + 1].astype(f32)
            )
            parts.append(6.0 * centre - (near + zsum(centre)))
        lap = jnp.concatenate(parts, axis=1)
        high = lap.astype(bf16)
        low = (lap - high.astype(f32)).astype(bf16)
        both = jnp.concatenate([high, low], axis=0)
        kap = row(kbuf, x + 1)

        @pl.loop(0, tiles, unroll=True)
        def _(it):
            at = at_tile(it)
            total = acc[x, at] + weighted(mix(it, both), kap)
            total = total - (w[x, at] + w[x + 2, at])
            centre = w[x + 1, at]
            sides = wy[x, at]
            for y in range(yl):
                here = slice(y * nz, (y + 1) * nz)
                below = sides[:, :nz] if y == 0 else centre[:, (y - 1) * nz:y * nz]
                above = sides[:, nz:] if y == yl - 1 else centre[:, (y + 1) * nz:(y + 2) * nz]
                value = total[:, here] - (below + above + zsum(centre[:, here]))
                store(y, at, (0.5 * value).astype(bf16))

    def out_copy(which, src, out, d, src_dev, srcx, dstx, width):
        return pltpu.make_async_remote_copy(
            src_ref=src(srcx, my_rows(d)),
            dst_ref=out.at[pl.ds((src_dev // group) * yl, yl), pl.ds((src_dev % group) * nx + dstx, width)],
            send_sem=out_send.at[which, d], recv_sem=out_recv.at[which, src_dev],
            device_id={"chaos": d}, device_id_type=MESH,
        )

    def own_copy(which, src, out, srcx, dstx, width):
        return pltpu.make_async_copy(
            src(srcx, my_rows(me)),
            out.at[pl.ds(band * yl, yl), pl.ds(part * nx + dstx, width)],
            local_sem.at[1 + which],
        )

    def out_start(which, src, out, srcx, dstx):
        @pl.loop(1, n)
        def _(s):
            out_copy(which, src, out, lax.rem(me + s, n), me, pl.ds(srcx, 1), dstx, 1).start()

        own_copy(which, src, out, pl.ds(srcx, 1), dstx, 1).start()

    def out_wait(which, src, out, srcx):
        @pl.loop(1, n)
        def _(s):
            d = lax.rem(me + s, n)
            copy = out_copy(which, src, out, d, d, srcx, 0, nx)
            copy.wait_send()
            copy.wait_recv()

        own_copy(which, src, out, srcx, 0, nx).wait()

    def first_at(xs, cs):
        return fbuf.at[rows, xs, cs]

    def second_at(xs, cs):
        return sbuf.at[:, xs, cs]

    @pl.loop(0, nx)
    def _(x):
        @pl.loop(1, n)
        def _(s):
            d = lax.rem(me + s, n)
            in_copy(d, d, x).wait_recv()

        own_in(x).wait()
        y_start(vbuf, vy_send, vy_recv, x + 1, x)
        x_start(vbuf, vh_send, vh_recv, 0, x == 0)
        x_start(vbuf, vh_send, vh_recv, 1, x == nx - 1)
        interior(vbuf, x)

    x_wait(vbuf, vh_send, vh_recv, 1)
    x_border(vbuf, 0)
    x_wait(vbuf, vh_send, vh_recv, 0)
    x_border(vbuf, nx + 1)

    @pl.loop(0, nx)
    def _(x):
        def store(y, at, value):
            fbuf[1 + y, x + 1, at] = value

        y_wait(vbuf, vy_send, vy_recv, x + 1, x)
        y_border(vbuf, x)
        finish(vbuf, x, store)
        y_start(fbuf, fy_send, fy_recv, x + 1, x)
        x_start(fbuf, fh_send, fh_recv, 0, x == 0)
        x_start(fbuf, fh_send, fh_recv, 1, x == nx - 1)
        out_start(0, first_at, out1, x + 1, x)

    interior(fbuf, 0)
    x_wait(fbuf, fh_send, fh_recv, 1)
    x_border(fbuf, 0)

    @pl.loop(0, nx)
    def _(x):
        def store(y, at, value):
            sbuf[y, x, at] = value

        @pl.when(x < nx - 1)
        def _():
            interior(fbuf, x + 1)

        @pl.when(x == nx - 1)
        def _():
            x_wait(fbuf, fh_send, fh_recv, 0)
            x_border(fbuf, nx + 1)

        y_wait(fbuf, fy_send, fy_recv, x + 1, x)
        y_border(fbuf, x)
        finish(fbuf, x, store)
        out_start(1, second_at, out2, x, x)

    @pl.loop(0, nx)
    def _(x):
        @pl.loop(1, n)
        def _(s):
            in_copy(lax.rem(me + s, n), me, x).wait_send()

        y_sent(vbuf, vy_send, vy_recv, x + 1, x)
        y_sent(fbuf, fy_send, fy_recv, x + 1, x)

    @pl.loop(1, group)
    def _(s):
        p = lax.rem(part + s, group)
        k_copy(p, part, band * group + p).wait_send()

    y_sent(kbuf, ky_send, ky_recv, inner, 0)
    x_sent(kbuf, kh_send, kh_recv)
    x_sent(vbuf, vh_send, vh_recv)
    x_sent(fbuf, fh_send, fh_recv)
    out_wait(0, first_at, out1, inner)
    out_wait(1, second_at, out2, pl.ds(0, nx))


def local(n, slabs, chaos_field, conductivity, triple_tensor, block_pattern):
    cl, slab, ny, nz = chaos_field.shape
    modes, coeffs, _ = triple_tensor.shape
    yl, nx, group = ny // BANDS, slab * BANDS // n, n // BANDS
    kpad = -(-modes // 8) * 8
    block = coeffs // block_pattern.shape[0]
    f32, bf16 = jnp.float32, jnp.bfloat16
    mask = jnp.repeat(jnp.repeat(block_pattern, block, 0), block, 1).astype(bf16)
    vt = jnp.transpose(chaos_field, (2, 1, 0, 3))
    kt = jnp.pad(jnp.transpose(conductivity, (2, 1, 0, 3)), ((0, 0), (0, 0), (0, kpad - modes), (0, 0)))
    dma, vmem = pltpu.SemaphoreType.DMA, pltpu.VMEM
    out = jax.ShapeDtypeStruct((ny, slab, cl, nz), bf16)
    whole = pl.BlockSpec(memory_space=pltpu.VMEM)
    anywhere = pl.BlockSpec(memory_space=pl.ANY)
    first, second = pl.pallas_call(
        functools.partial(kernel, n, slabs, modes),
        out_shape=(out, out),
        in_specs=[anywhere, whole, whole, anywhere],
        out_specs=(anywhere, anywhere),
        scratch_shapes=[
            vmem((yl + 2, nx + 2, coeffs, nz), bf16),
            vmem((yl + 2, nx + 2, coeffs, nz), bf16),
            vmem((yl, nx, coeffs, nz), bf16),
            vmem((yl + 2, nx + 2, kpad, nz), f32),
            vmem((nx, kpad, yl * nz), f32),
            vmem((coeffs // TILE, modes * TILE, 2 * coeffs), bf16),
            vmem((nx, coeffs, yl * nz), f32),
            vmem((nx + 2, coeffs, yl * nz), f32),
            vmem((nx, coeffs, 2 * nz), f32),
            dma((nx, n)), dma((nx, n)), dma((nx,)), dma((group,)), dma((group,)),
            dma((2, 1)), dma((2, 1)), dma((2, nx)), dma((2, nx)), dma((2, nx)), dma((2, nx)),
            dma((2,)), dma((2,)), dma((2,)), dma((2,)), dma((2,)), dma((2,)),
            dma((2, n)), dma((2, n)), dma((3,)),
        ],
        compiler_params=pltpu.CompilerParams(
            collective_id=0, has_side_effects=True, vmem_limit_bytes=48 * 1024 * 1024,
        ),
    )(vt, triple_tensor, mask, kt)
    return jnp.transpose(first, (2, 1, 0, 3)), jnp.transpose(second, (2, 1, 0, 3))


def solution(mesh):
    n, slabs = mesh.shape["chaos"], mesh.shape["space"]
    return jax.shard_map(
        functools.partial(local, n, slabs),
        mesh=mesh,
        in_specs=(P("chaos", "space", None, None), P(None, "space", "chaos", None), P(), P()),
        out_specs=(P("chaos", "space", None, None), P("chaos", "space", None, None)),
        check_vma=False,
    )
```
